32 devices in a mesh: dp: 4 (over x, core), expert: 8 (over z, y).
Axes of the slice: x: 2, y: 2, z: 4, core: 2. Of those that a mesh axis runs over, the one named last changes fastest.
Arguments:
- tokens: bfloat16 [128, 7168], P(('dp', 'expert')), may hold values from -6 to 6
- routes: int32 [128, 8], P(('dp', 'expert')), may hold values from 0 to 31, all different within a row; in each aligned block of 4 rows (0 to 3, 4 to 7, ...) at most 2 rows name the same one
- gate_scores: float32 [128, 8], P(('dp', 'expert')), may hold values from 0.1 to 1
- w_gate: bfloat16 [32, 7168, 2048], P('expert', None, 'dp'), may hold values from -0.0625 to 0.0625
- w_up: bfloat16 [32, 7168, 2048], P('expert', None, 'dp'), may hold values from -0.0625 to 0.0625
- w_down: bfloat16 [32, 2048, 7168], P('expert', None, 'dp'), may hold values from -0.125 to 0.125
Outputs:
- combined: bfloat16 [128, 7168], P(('dp', 'expert'))
The draws below stay inside these ranges and needn't reach their ends.
Inputs may be any that keep to these rules, and one draw needn't show every extreme that they name: `routes`: each row names 8 different experts; among the rows of one device no expert is named more than 2 times, a bound that some block reaches.
All inputs are finite; a program needn't handle non-finite values.
Results may differ from the reference program's by a relative error of at most 0.0057.
Values may be sent and summed in bfloat16 or wider, within the bound.
A program may use at most 192 MiB of HBM per device.

```python
import math
import jax
import jax.numpy as jnp
import numpy as np
from jax import lax

D = 7168
FF = 2048
TOPK = 8
E = 32
TOK_DEV = 4
CAP = 2
TOKENS = 128
DEVICES = 32


def shard_levels(rng, shape, cuts, smallest, largest):
    level = 1.0
    for position, shards_of in cuts:
        heights = jax.random.uniform(jax.random.fold_in(jax.random.fold_in(rng, 6), position), (shards_of,), jnp.float32, smallest / len(cuts), largest / len(cuts))
        level = level * jnp.repeat(jnp.exp(heights), shape[position] // shards_of).reshape((-1,) + (1,) * (len(shape) - 1 - position))
    return level


def routed_block(stream_key, own, number, rows, number_of, top, most, slope):
    sequence = jax.random.permutation(stream_key, number_of)
    heavy_load, ordinary = shares(number_of, rows * top, most, slope, True), shares(number_of, rows * top, most, slope, False)
    places = jnp.arange(number_of)

    def named(lengths, rotation):
        used = int((lengths > 0).sum())
        fixed = max(1, used // 4)
        moved = fixed + (places - fixed + rotation * (used - fixed)) % max(1, number_of - fixed)
        return jnp.zeros((number_of,), jnp.int32).at[sequence[jnp.where(places < fixed, places, moved)]].set(jnp.asarray(lengths, jnp.int32))

    lengths = jnp.where(number % 4 == 0, named(heavy_load, number // 4), named(ordinary, number - number // 4 - 1))
    mixed = jax.random.permutation(jax.random.fold_in(own, 3), number_of)
    giver, sink = mixed[0:number_of // 2 * 2:2], mixed[1:number_of // 2 * 2:2]
    slack = jnp.minimum(lengths[giver] - 1, most - lengths[sink]) // 2
    slack = jnp.where((giver == sequence[0]) | (sink == sequence[0]) | (lengths[sink] == 0), 0, jnp.maximum(slack, 0))
    moved = jax.random.randint(jax.random.fold_in(own, 4), (number_of // 2,), 0, 1 << 20) % (slack + 1)
    lengths = lengths.at[giver].add(-moved).at[sink].add(moved)
    items = jnp.searchsorted(jnp.cumsum(lengths), jnp.arange(rows * top), side="right").astype(jnp.int32)
    grid = items.reshape(top, rows).T
    grid = grid[jax.random.permutation(jax.random.fold_in(own, 1), rows)]
    rotation = jax.random.randint(jax.random.fold_in(own, 2), (rows, 1), 0, top)
    return jnp.take_along_axis(grid, (jnp.arange(top)[None, :] + rotation) % top, axis=1)


def shares(number_of, total, reach, slope, full):
    portions = [(1 << 20) // math.isqrt(standing ** slope) + 1 for standing in range(1, number_of + 1)]
    largest = reach if full else min(reach, max(-(-total // number_of), total * portions[0] // sum(portions)))
    least = 1 if total - largest >= number_of - 1 else 0
    holding, rest = [largest] + [least] * (number_of - 1), total - largest - least * (number_of - 1)
    while rest > 0:
        candidates = [i for i in range(1, number_of) if holding[i] < largest] or [i for i in range(1, number_of) if holding[i] < reach]
        mass, left = sum([portions[i] for i in candidates]), rest
        for i in candidates:
            extra = min(reach - holding[i], max(1, left * portions[i] // mass), rest)
            holding[i] = holding[i] + extra
            rest = rest - extra
    return np.array(holding)


def noise(stream_key, dims, deviation, limit, split=(), held_as=jnp.bfloat16):
    level = shard_levels(stream_key, dims, split, -0.22, 0.18) if split else 1.0
    entries = jax.random.normal(stream_key, dims, jnp.float32) * deviation * level
    return jnp.minimum(jnp.maximum(entries, -limit), limit).astype(held_as)


def setup_inputs(seed: int = 0) -> dict:
    arg_keys = jax.random.split(jax.random.key(seed), 7)
    tokens = noise(arg_keys[0], (TOKENS, D), 1.0, 6.0, ((0, 32),))
    routes_keys = jax.random.split(jax.random.fold_in(arg_keys[1], 1), TOKENS // TOK_DEV)
    routes_turns = jax.random.permutation(jax.random.fold_in(arg_keys[1], 3), TOKENS // TOK_DEV)
    routes = jax.vmap(lambda own, number: routed_block(jax.random.fold_in(arg_keys[1], 2), own, number, TOK_DEV, E, TOPK, CAP, 2))(routes_keys, routes_turns).reshape((TOKENS, TOPK))
    gate_scores = jnp.clip(0.1 + 0.9 * jax.random.uniform(arg_keys[2], (TOKENS, TOPK), jnp.float32) ** shard_levels(arg_keys[2], (TOKENS, TOPK), ((0, 32),), -0.2, 0.2), 0.1, 1.0)
    w_gate = noise(arg_keys[3], (E, D, FF), D ** -0.5, 0.0625, ((0, 8), (2, 4)))
    w_up = noise(arg_keys[4], (E, D, FF), D ** -0.5, 0.0625, ((0, 8), (2, 4)))
    w_down = noise(arg_keys[5], (E, FF, D), FF ** -0.5, 0.125, ((0, 8), (2, 4)))
    return dict(tokens=tokens, routes=routes, gate_scores=gate_scores, w_gate=w_gate, w_up=w_up, w_down=w_down)


def slot_codes(route_block):
    route_list = route_block.reshape(-1)
    onehot = (route_list[:, None] == jnp.arange(E, dtype=jnp.int32)[None, :]).astype(jnp.int32)
    before = jnp.cumsum(onehot, axis=0) - onehot
    return jnp.sum(before * onehot, axis=1).astype(jnp.int32)


def reference(tokens, routes, gate_scores, w_gate, w_up, w_down):
    blocks = routes.reshape(DEVICES, TOK_DEV, TOPK)
    slots = jax.vmap(slot_codes)(blocks).reshape(-1)
    pair_ids = jnp.arange(TOKENS * TOPK, dtype=jnp.int32)
    source = pair_ids // (TOK_DEV * TOPK)
    token_of = pair_ids // TOPK
    expert_of = routes.reshape(-1)
    row_of = (source * CAP + slots).astype(jnp.int32)
    table = jnp.zeros((E, DEVICES * CAP), jnp.int32).at[expert_of, row_of].set(token_of)

    def one_expert(packed):
        row_ids, gate_mat, up_mat, down_mat = packed
        inputs = tokens[row_ids].astype(jnp.float32)
        gate_part = jnp.dot(inputs, gate_mat.astype(jnp.float32), precision=lax.Precision.HIGHEST)
        up_part = jnp.dot(inputs, up_mat.astype(jnp.float32), precision=lax.Precision.HIGHEST)
        hidden = (jax.nn.silu(gate_part) * up_part).astype(jnp.bfloat16)
        result = jnp.dot(hidden.astype(jnp.float32), down_mat.astype(jnp.float32), precision=lax.Precision.HIGHEST)
        return result.astype(jnp.bfloat16)

    expert_out = lax.map(one_expert, (table, w_gate, w_up, w_down))
    picked = expert_out[expert_of, row_of].astype(jnp.float32).reshape(TOKENS, TOPK, D)
    combined = jnp.sum(picked * gate_scores[:, :, None], axis=1)
    return combined.astype(jnp.bfloat16)
```

```python
import functools

import jax
import jax.numpy as jnp
from jax import lax
from jax.experimental import pallas as pl
from jax.experimental.pallas import tpu as pltpu
from jax.sharding import PartitionSpec as P

MESH = pl.DeviceIdType.MESH
F32, BF16 = jnp.float32, jnp.bfloat16
PARTS = 4
CHUNKS = 7
LANES = 128

ORDERS = (("a", "b", "x", "c"), ("x", "b", "a", "c"))


def kernel(
    sizes, ring, down_ring,
    tokens, routes, scores, w_gate, w_up, w_down, out,
    g0, g1, rows, score, weights, acc, hidden, down, total, sent, arrived, fin, fin_in,
    tok_send, tok_recv, w_sem, d_sem, h_send, h_recv, r_send, r_recv, f_send, f_recv,
):
    n = dict(zip("abxc", sizes))
    n_dp, n_e = n["x"] * n["c"], n["a"] * n["b"]
    tok, width = tokens.shape
    local, _, ff = w_gate.shape
    slab = width // PARTS
    half = slab // 2
    group = n_dp * tok
    count = n_e * group
    chunk = w_down.shape[2] // CHUNKS
    steps = local * PARTS

    dp, ex = lax.axis_index("dp"), lax.axis_index("expert")
    me = dict(a=ex // n["b"], b=lax.rem(ex, n["b"]), x=dp // n["c"], c=lax.rem(dp, n["c"]))

    def device(at):
        return (at["x"] * n["c"] + at["c"], at["a"] * n["b"] + at["b"])

    def w_copies(i):
        e, q, slot = i // PARTS, lax.rem(i, PARTS), lax.rem(i, ring)
        part = pl.ds(pl.multiple_of(q * slab, slab), slab)
        return [
            pltpu.make_async_copy(w.at[e, part, :], weights.at[slot, j], w_sem.at[slot, j])
            for j, w in enumerate((w_gate, w_up))
        ]

    def d_copy(i):
        slot = lax.rem(i, down_ring)
        columns = pl.ds(pl.multiple_of(i * chunk, chunk), chunk)
        return pltpu.make_async_copy(w_down.at[:, :, columns], down.at[slot], d_sem.at[slot])

    @pl.loop(0, ring)
    def _(i):
        for copy in w_copies(i):
            copy.start()

    barrier = pltpu.get_barrier_semaphore()
    for k in range(1, n_dp):
        pl.semaphore_signal(barrier, inc=1, device_id=(lax.rem(dp + k, n_dp), ex), device_id_type=MESH)

    @pl.loop(1, n_e)
    def _(k):
        pl.semaphore_signal(barrier, inc=1, device_id=(dp, lax.rem(ex + k, n_e)), device_id_type=MESH)

    t32 = tokens[...].astype(F32)
    lanes = lax.broadcasted_iota(jnp.int32, (tok, LANES), 1)
    dense = jnp.zeros((tok, LANES), F32)
    for k in range(routes.shape[1]):
        dense += jnp.where(lanes == routes[:, k : k + 1], scores[:, k : k + 1], 0.0)
    terms, rest = [], dense
    for _ in range(3):
        term = rest.astype(BF16).astype(F32)
        terms.append(term)
        rest = rest - term
    terms.append(jnp.zeros((tok, LANES), F32))
    own = (me["a"], me["b"], me["x"], me["c"])
    cut = [t32[:, q * slab : (q + 1) * slab] for q in range(PARTS)]
    g0[own + (slice(None), slice(0, half))] = jnp.concatenate([p[:, :half] for p in cut], 0).astype(BF16)
    g0[own + (slice(None), slice(half, half + LANES))] = jnp.concatenate(terms, 0).astype(BF16)
    g1[own] = jnp.concatenate([p[:, half:] for p in cut], 0).astype(BF16)

    pl.semaphore_wait(barrier, n_dp - 1 + n_e - 1)

    def gather_copies(stream, stage):
        order, buf = ORDERS[stream], (g0, g1)[stream]
        axis = order[stage]
        at = tuple(slice(None) if d in order[:stage] else me[d] for d in "abxc")
        made = []
        for k in range(1, n[axis]):
            peer = dict(me)
            peer[axis] = lax.rem(me[axis] + k, n[axis])
            made.append(pltpu.make_async_remote_copy(
                src_ref=buf.at[at], dst_ref=buf.at[at],
                send_sem=tok_send.at[stream, stage, k], recv_sem=tok_recv.at[stream, stage, k],
                device_id=device(peer), device_id_type=MESH,
            ))
        return made

    for stage in range(4):
        for stream in range(2):
            if stage:
                for copy in gather_copies(stream, stage - 1):
                    copy.wait_recv()
            for copy in gather_copies(stream, stage):
                copy.start()
    for stream in range(2):
        for copy in gather_copies(stream, 3):
            copy.wait_recv()

    size = n_dp * PARTS * tok
    to = lax.broadcasted_iota(jnp.int32, (size, size), 0)
    came = lax.broadcasted_iota(jnp.int32, (size, size), 1)
    part, block, token = to // group, lax.rem(to, group) // tok, lax.rem(to, tok)
    perm = (came == (block * PARTS + part) * tok + token).astype(F32).astype(BF16)

    @pl.loop(0, n_e)
    def _(e):
        a, b = e // n["b"], lax.rem(e, n["b"])
        first = jnp.dot(perm, g0[a, b].reshape(size, half + LANES), preferred_element_type=F32)
        second = jnp.dot(perm, g1[a, b].reshape(size, half), preferred_element_type=F32)
        at = pl.ds(pl.multiple_of(e * group, group), group)
        for q in range(PARTS):
            mine = slice(q * group, (q + 1) * group)
            rows[q, at, 0:half] = first[mine, :half].astype(BF16)
            rows[q, at, half:slab] = second[mine].astype(BF16)
        s = [first[q * group : (q + 1) * group, half:] for q in range(3)]
        score[at, :] = s[0] + s[1] + s[2]

    tile = min(count, 128)

    def tiles(body):
        if count == tile:
            body(pl.ds(0, tile))
        else:
            @pl.loop(0, count // tile)
            def _(m):
                body(pl.ds(pl.multiple_of(m * tile, tile), tile))

    other = dict(me)
    other["c"] = lax.rem(me["c"] + 1, n["c"])

    def h_copy(e, block, peer, k):
        return pltpu.make_async_remote_copy(
            src_ref=hidden.at[e, block], dst_ref=hidden.at[e, block],
            send_sem=h_send.at[e, k], recv_sem=h_recv.at[e, k],
            device_id=device(peer), device_id_type=MESH,
        )

    def h_along_x(e):
        made = []
        for k in range(1, n["x"]):
            peer = dict(me)
            peer["x"] = lax.rem(me["x"] + k, n["x"])
            made.append(h_copy(e, dp, peer, k))
        return made

    def h_across(e, k):
        x = lax.rem(me["x"] + n["x"] - k, n["x"])
        return h_copy(e, x * n["c"] + me["c"], other, n["x"] + k)

    def forward(e):
        for k, copy in enumerate(h_along_x(e), 1):
            copy.wait_recv()
            h_across(e, k).start()

    @pl.loop(0, local)
    def _(e):
        @pl.loop(0, PARTS)
        def _(q):
            i = e * PARTS + q
            slot = lax.rem(i, ring)
            for copy in w_copies(i):
                copy.wait()

            def multiply(at):
                for j in range(2):
                    part = jnp.dot(rows[q, at, :], weights[slot, j], preferred_element_type=F32)
                    acc[j, at, :] = jnp.where(q == 0, 0.0, acc[j, at, :]) + part

            tiles(multiply)

            @pl.when(i + ring < steps)
            def _():
                for copy in w_copies(i + ring):
                    copy.start()

            @pl.when(jnp.logical_and(i + ring >= steps, i + ring - steps < down_ring))
            def _():
                d_copy(i + ring - steps).start()

        def activate(at):
            gate, up = acc[0, at, :], acc[1, at, :]
            mask = lax.broadcasted_iota(jnp.int32, (tile, LANES), 1) == ex * local + e
            weight = jnp.sum(jnp.where(mask, score[at, :], 0.0), axis=1, keepdims=True)
            hidden[e, dp, at, :] = (gate / (1.0 + jnp.exp(-gate)) * up * weight).astype(BF16)

        tiles(activate)
        for copy in h_along_x(e):
            copy.start()
        h_across(e, 0).start()

        @pl.when(e > 0)
        def _():
            forward(e - 1)

    forward(local - 1)

    def r_copy(c, k):
        return pltpu.make_async_remote_copy(
            src_ref=sent.at[c, lax.rem(ex + k, n_e)], dst_ref=arrived.at[c, k - 1],
            send_sem=r_send.at[c], recv_sem=r_recv.at[c],
            device_id=(dp, lax.rem(ex + k, n_e)), device_id_type=MESH,
        )

    @pl.loop(0, CHUNKS)
    def _(c):
        slot = lax.rem(c, down_ring)
        d_copy(c).wait()

        @pl.loop(0, local)
        def _(e):
            @pl.when(c == 0)
            def _():
                for k in range(n["x"]):
                    h_across(e, k).wait_recv()

            def multiply(at):
                part = jnp.where(e == 0, 0.0, total[at, :])
                for p in range(n_dp):
                    part += jnp.dot(
                        hidden[e, p, at, :], down[slot, e, p * ff : (p + 1) * ff, :],
                        preferred_element_type=F32,
                    )
                total[at, :] = part

            tiles(multiply)

        @pl.when(c + down_ring < CHUNKS)
        def _():
            d_copy(c + down_ring).start()

        @pl.loop(0, n_e)
        def _(k):
            sent[c, k] = total[pl.ds(pl.multiple_of(k * group, group), group), :].astype(BF16)

        @pl.loop(1, n_e)
        def _(k):
            r_copy(c, k).start()

    def f_copy(k):
        to = lax.rem(dp + k, n_dp)
        return pltpu.make_async_remote_copy(
            src_ref=fin.at[to], dst_ref=fin_in.at[k],
            send_sem=f_send.at[k], recv_sem=f_recv.at[k],
            device_id=(to, ex), device_id_type=MESH,
        )

    for c in range(CHUNKS):
        pltpu.make_async_copy(arrived.at[c], arrived.at[c], r_recv.at[c]).wait()
        value = sent[c, ex].astype(F32)
        for k in range(n_e - 1):
            value += arrived[c, k].astype(F32)
        for p in range(n_dp):
            fin[p, :, c * chunk : (c + 1) * chunk] = value[p * tok : (p + 1) * tok]
    for k in range(1, n_dp):
        f_copy(k).start()
    span = w_down.shape[2]
    for k in range(n_dp):
        came_from = lax.rem(dp + n_dp - k, n_dp)
        if k:
            f_copy(k).wait_recv()
        value = fin_in[k] if k else fin[dp]
        out[:, pl.ds(pl.multiple_of(came_from * span, LANES), span)] = value.astype(BF16)

    for stage in range(4):
        for stream in range(2):
            for copy in gather_copies(stream, stage):
                copy.wait_send()

    @pl.loop(0, local)
    def _(e):
        for copy in h_along_x(e):
            copy.wait_send()
        for k in range(n["x"]):
            h_across(e, k).wait_send()

    @pl.loop(0, CHUNKS)
    def _(c):
        pltpu.make_async_copy(arrived.at[c], arrived.at[c], r_send.at[c]).wait()

    for k in range(1, n_dp):
        f_copy(k).wait_send()


def body(tokens, routes, gate_scores, w_gate, w_up, w_down):
    n_dp, n_e = lax.axis_size("dp"), lax.axis_size("expert")
    sizes = (4, n_e // 4, n_dp // 2, 2)
    tok, width = tokens.shape
    local, _, ff = w_gate.shape
    slab, half = width // PARTS, width // PARTS // 2
    group = n_dp * tok
    count = n_e * group
    depth, span = w_down.shape[1:]
    chunk = span // CHUNKS
    ring = min(9, local * PARTS)
    down_ring = 4
    ring = max(ring, down_ring)
    sem = pltpu.SemaphoreType.DMA
    vmem = pl.BlockSpec(memory_space=pltpu.VMEM)
    hbm = pl.BlockSpec(memory_space=pl.ANY)
    return pl.pallas_call(
        functools.partial(kernel, sizes, ring, down_ring),
        out_shape=jax.ShapeDtypeStruct((tok, width), BF16),
        in_specs=[vmem] * 3 + [hbm] * 3,
        out_specs=vmem,
        scratch_shapes=[
            pltpu.VMEM(sizes + (PARTS * tok, half + LANES), BF16),
            pltpu.VMEM(sizes + (PARTS * tok, half), BF16),
            pltpu.VMEM((PARTS, count, slab), BF16),
            pltpu.VMEM((count, LANES), F32),
            pltpu.VMEM((ring, 2, slab, ff), BF16),
            pltpu.VMEM((2, count, ff), F32),
            pltpu.VMEM((local, n_dp, count, ff), BF16),
            pltpu.VMEM((down_ring, local, depth, chunk), BF16),
            pltpu.VMEM((count, chunk), F32),
            pltpu.VMEM((CHUNKS, n_e, group, chunk), BF16),
            pltpu.VMEM((CHUNKS, n_e - 1, group, chunk), BF16),
            pltpu.VMEM((n_dp, tok, span), F32),
            pltpu.VMEM((n_dp, tok, span), F32),
            sem((2, 4, max(sizes))), sem((2, 4, max(sizes))),
            sem((ring, 2)), sem((down_ring,)),
            sem((local, 2 * sizes[2])), sem((local, 2 * sizes[2])),
            sem((CHUNKS,)), sem((CHUNKS,)),
            sem((n_dp,)), sem((n_dp,)),
        ],
        compiler_params=pltpu.CompilerParams(
            collective_id=0, has_side_effects=True, vmem_limit_bytes=62 * 2**20
        ),
    )(tokens, routes, gate_scores, w_gate, w_up, w_down)


def solution(mesh):
    placed = (
        P(("dp", "expert"), None),
        P(("dp", "expert"), None),
        P(("dp", "expert"), None),
        P("expert", None, "dp"),
        P("expert", None, "dp"),
        P("expert", None, "dp"),
    )
    return jax.shard_map(
        body, mesh=mesh, in_specs=placed, out_specs=P(("dp", "expert"), None), check_vma=False
    )
```

```python
import functools

import jax
import jax.numpy as jnp
from jax import lax
from jax.experimental import pallas as pl
from jax.experimental.pallas import tpu as pltpu
from jax.sharding import PartitionSpec as P

MESH = pl.DeviceIdType.MESH
F32, BF16 = jnp.float32, jnp.bfloat16
PARTS = 4
CHUNKS = 7
LANES = 128

ORDERS = (('a', 'b', 'x', 'c'), ('a', 'x', 'b', 'c'))


def kernel(
    sizes, ring, down_ring,
    tokens, routes, scores, w_gate, w_up, w_down, out,
    g0, g1, rows, score, weights, acc, hidden, down, total, sent, arrived, fin, fin_in,
    tok_send, tok_recv, w_sem, d_sem, h_send, h_recv, r_send, r_recv, f_send, f_recv,
):
    n = dict(zip("abxc", sizes))
    n_dp, n_e = n["x"] * n["c"], n["a"] * n["b"]
    tok, width = tokens.shape
    local, _, ff = w_gate.shape
    slab = width // PARTS
    half = slab // 2
    group = n_dp * tok
    count = n_e * group
    chunk = w_down.shape[2] // CHUNKS
    steps = local * PARTS

    dp, ex = lax.axis_index("dp"), lax.axis_index("expert")
    me = dict(a=ex // n["b"], b=lax.rem(ex, n["b"]), x=dp // n["c"], c=lax.rem(dp, n["c"]))

    def device(at):
        return (at["x"] * n["c"] + at["c"], at["a"] * n["b"] + at["b"])

    def w_copies(i):
        e, q, slot = i // PARTS, lax.rem(i, PARTS), lax.rem(i, ring)
        part = pl.ds(pl.multiple_of(q * slab, slab), slab)
        return [
            pltpu.make_async_copy(w.at[e, part, :], weights.at[slot, j], w_sem.at[slot, j])
            for j, w in enumerate((w_gate, w_up))
        ]

    def d_copy(i):
        slot = lax.rem(i, down_ring)
        columns = pl.ds(pl.multiple_of(i * chunk, chunk), chunk)
        return pltpu.make_async_copy(w_down.at[:, :, columns], down.at[slot], d_sem.at[slot])

    @pl.loop(0, ring)
    def _(i):
        for copy in w_copies(i):
            copy.start()

    @pl.loop(0, down_ring)
    def _(i):
        d_copy(i).start()

    barrier = pltpu.get_barrier_semaphore()
    for k in range(1, n_dp):
        pl.semaphore_signal(barrier, inc=1, device_id=(lax.rem(dp + k, n_dp), ex), device_id_type=MESH)

    @pl.loop(1, n_e)
    def _(k):
        pl.semaphore_signal(barrier, inc=1, device_id=(dp, lax.rem(ex + k, n_e)), device_id_type=MESH)

    t32 = tokens[...].astype(F32)
    lanes = lax.broadcasted_iota(jnp.int32, (tok, LANES), 1)
    dense = jnp.zeros((tok, LANES), F32)
    for k in range(routes.shape[1]):
        dense += jnp.where(lanes == routes[:, k : k + 1], scores[:, k : k + 1], 0.0)
    terms, rest = [], dense
    for _ in range(3):
        term = rest.astype(BF16).astype(F32)
        terms.append(term)
        rest = rest - term
    terms.append(jnp.zeros((tok, LANES), F32))
    own = (me["a"], me["b"], me["x"], me["c"])
    cut = [t32[:, q * slab : (q + 1) * slab] for q in range(PARTS)]
    g0[own + (slice(None), slice(0, half))] = jnp.concatenate([p[:, :half] for p in cut], 0).astype(BF16)
    g0[own + (slice(None), slice(half, half + LANES))] = jnp.concatenate(terms, 0).astype(BF16)
    g1[own] = jnp.concatenate([p[:, half:] for p in cut], 0).astype(BF16)

    pl.semaphore_wait(barrier, n_dp - 1 + n_e - 1)

    def gather_copies(stream, stage):
        order, buf = ORDERS[stream], (g0, g1)[stream]
        axis = order[stage]
        at = tuple(slice(None) if d in order[:stage] else me[d] for d in "abxc")
        made = []
        for k in range(1, n[axis]):
            peer = dict(me)
            peer[axis] = lax.rem(me[axis] + k, n[axis])
            made.append(pltpu.make_async_remote_copy(
                src_ref=buf.at[at], dst_ref=buf.at[at],
                send_sem=tok_send.at[stream, stage, k], recv_sem=tok_recv.at[stream, stage, k],
                device_id=device(peer), device_id_type=MESH,
            ))
        return made

    for stage in range(4):
        for stream in range(2):
            if stage:
                for copy in gather_copies(stream, stage - 1):
                    copy.wait_recv()
            for copy in gather_copies(stream, stage):
                copy.start()
    for stream in range(2):
        for copy in gather_copies(stream, 3):
            copy.wait_recv()

    size = n_dp * PARTS * tok
    to = lax.broadcasted_iota(jnp.int32, (size, size), 0)
    came = lax.broadcasted_iota(jnp.int32, (size, size), 1)
    part, block, token = to // group, lax.rem(to, group) // tok, lax.rem(to, tok)
    perm = (came == (block * PARTS + part) * tok + token).astype(F32).astype(BF16)

    @pl.loop(0, n_e)
    def _(e):
        a, b = e // n["b"], lax.rem(e, n["b"])
        first = jnp.dot(perm, g0[a, b].reshape(size, half + LANES), preferred_element_type=F32)
        second = jnp.dot(perm, g1[a, b].reshape(size, half), preferred_element_type=F32)
        at = pl.ds(pl.multiple_of(e * group, group), group)
        for q in range(PARTS):
            mine = slice(q * group, (q + 1) * group)
            rows[q, at, 0:half] = first[mine, :half].astype(BF16)
            rows[q, at, half:slab] = second[mine].astype(BF16)
        s = [first[q * group : (q + 1) * group, half:] for q in range(3)]
        score[at, :] = s[0] + s[1] + s[2]

    tile = min(count, 128)

    def tiles(body):
        if count == tile:
            body(pl.ds(0, tile))
        else:
            @pl.loop(0, count // tile)
            def _(m):
                body(pl.ds(pl.multiple_of(m * tile, tile), tile))

    other = dict(me)
    other["c"] = lax.rem(me["c"] + 1, n["c"])

    def h_copy(e, block, peer, k):
        return pltpu.make_async_remote_copy(
            src_ref=hidden.at[e, block], dst_ref=hidden.at[e, block],
            send_sem=h_send.at[e, k], recv_sem=h_recv.at[e, k],
            device_id=device(peer), device_id_type=MESH,
        )

    def h_along_x(e):
        made = []
        for k in range(1, n["x"]):
            peer = dict(me)
            peer["x"] = lax.rem(me["x"] + k, n["x"])
            made.append(h_copy(e, dp, peer, k))
        return made

    def h_across(e, k):
        x = lax.rem(me["x"] + n["x"] - k, n["x"])
        return h_copy(e, x * n["c"] + me["c"], other, n["x"] + k)

    def forward(e):
        for k, copy in enumerate(h_along_x(e), 1):
            copy.wait_recv()
            h_across(e, k).start()

    @pl.loop(0, local)
    def _(e):
        @pl.loop(0, PARTS)
        def _(q):
            i = e * PARTS + q
            slot = lax.rem(i, ring)
            for copy in w_copies(i):
                copy.wait()

            def multiply(at):
                for j in range(2):
                    part = jnp.dot(rows[q, at, :], weights[slot, j], preferred_element_type=F32)
                    acc[j, at, :] = jnp.where(q == 0, 0.0, acc[j, at, :]) + part

            tiles(multiply)

            @pl.when(i + ring < steps)
            def _():
                for copy in w_copies(i + ring):
                    copy.start()

        def activate(at):
            gate, up = acc[0, at, :], acc[1, at, :]
            mask = lax.broadcasted_iota(jnp.int32, (tile, LANES), 1) == ex * local + e
            weight = jnp.sum(jnp.where(mask, score[at, :], 0.0), axis=1, keepdims=True)
            hidden[e, dp, at, :] = (gate / (1.0 + jnp.exp(-gate)) * up * weight).astype(BF16)

        tiles(activate)
        for copy in h_along_x(e):
            copy.start()
        h_across(e, 0).start()

        @pl.when(e > 0)
        def _():
            forward(e - 1)

    def r_copy(c, k):
        return pltpu.make_async_remote_copy(
            src_ref=sent.at[c, lax.rem(ex + k, n_e)], dst_ref=arrived.at[c, k - 1],
            send_sem=r_send.at[c], recv_sem=r_recv.at[c],
            device_id=(dp, lax.rem(ex + k, n_e)), device_id_type=MESH,
        )

    def project(c, e, first):
        slot = lax.rem(c, down_ring)

        def multiply(at):
            part = jnp.where(first, 0.0, total[slot, at, :])
            for p in range(n_dp):
                part += jnp.dot(
                    hidden[e, p, at, :], down[slot, e, p * ff : (p + 1) * ff, :],
                    preferred_element_type=F32,
                )
            total[slot, at, :] = part

        tiles(multiply)

    before = local - 1

    @pl.loop(0, down_ring)
    def _(c):
        d_copy(c).wait()

        @pl.loop(0, before)
        def _(e):
            @pl.when(c == 0)
            def _():
                for k in range(n["x"]):
                    h_across(e, k).wait_recv()

            project(c, e, e == 0)

        @pl.when(c == min(1, down_ring - 1))
        def _():
            forward(local - 1)

    for k in range(n["x"]):
        h_across(local - 1, k).wait_recv()

    @pl.loop(0, CHUNKS)
    def _(c):
        slot = lax.rem(c, down_ring)

        @pl.when(c >= down_ring)
        def _():
            d_copy(c).wait()

            @pl.loop(0, before)
            def _(e):
                project(c, e, e == 0)

        project(c, before, before == 0)

        @pl.when(c + down_ring < CHUNKS)
        def _():
            d_copy(c + down_ring).start()

        @pl.loop(0, n_e)
        def _(k):
            sent[c, k] = total[slot, pl.ds(pl.multiple_of(k * group, group), group), :].astype(BF16)

        @pl.loop(1, n_e)
        def _(k):
            r_copy(c, k).start()

    def f_copy(k):
        to = lax.rem(dp + k, n_dp)
        return pltpu.make_async_remote_copy(
            src_ref=fin.at[to], dst_ref=fin_in.at[k],
            send_sem=f_send.at[k], recv_sem=f_recv.at[k],
            device_id=(to, ex), device_id_type=MESH,
        )

    for c in range(CHUNKS):
        pltpu.make_async_copy(arrived.at[c], arrived.at[c], r_recv.at[c]).wait()
        value = sent[c, ex].astype(F32)
        for k in range(n_e - 1):
            value += arrived[c, k].astype(F32)
        for p in range(n_dp):
            fin[p, :, c * chunk : (c + 1) * chunk] = value[p * tok : (p + 1) * tok]
    for k in range(1, n_dp):
        f_copy(k).start()
    span = w_down.shape[2]
    for k in range(n_dp):
        came_from = lax.rem(dp + n_dp - k, n_dp)
        if k:
            f_copy(k).wait_recv()
        value = fin_in[k] if k else fin[dp]
        out[:, pl.ds(pl.multiple_of(came_from * span, LANES), span)] = value.astype(BF16)

    for stage in range(4):
        for stream in range(2):
            for copy in gather_copies(stream, stage):
                copy.wait_send()

    @pl.loop(0, local)
    def _(e):
        for copy in h_along_x(e):
            copy.wait_send()
        for k in range(n["x"]):
            h_across(e, k).wait_send()

    @pl.loop(0, CHUNKS)
    def _(c):
        pltpu.make_async_copy(arrived.at[c], arrived.at[c], r_send.at[c]).wait()

    for k in range(1, n_dp):
        f_copy(k).wait_send()


def body(tokens, routes, gate_scores, w_gate, w_up, w_down):
    n_dp, n_e = lax.axis_size("dp"), lax.axis_size("expert")
    sizes = (4, n_e // 4, n_dp // 2, 2)
    tok, width = tokens.shape
    local, _, ff = w_gate.shape
    slab, half = width // PARTS, width // PARTS // 2
    group = n_dp * tok
    count = n_e * group
    depth, span = w_down.shape[1:]
    chunk = span // CHUNKS
    ring = min(9, local * PARTS)
    down_ring = 4
    sem = pltpu.SemaphoreType.DMA
    vmem = pl.BlockSpec(memory_space=pltpu.VMEM)
    hbm = pl.BlockSpec(memory_space=pl.ANY)
    return pl.pallas_call(
        functools.partial(kernel, sizes, ring, down_ring),
        out_shape=jax.ShapeDtypeStruct((tok, width), BF16),
        in_specs=[vmem] * 3 + [hbm] * 3,
        out_specs=vmem,
        scratch_shapes=[
            pltpu.VMEM(sizes + (PARTS * tok, half + LANES), BF16),
            pltpu.VMEM(sizes + (PARTS * tok, half), BF16),
            pltpu.VMEM((PARTS, count, slab), BF16),
            pltpu.VMEM((count, LANES), F32),
            pltpu.VMEM((ring, 2, slab, ff), BF16),
            pltpu.VMEM((2, count, ff), F32),
            pltpu.VMEM((local, n_dp, count, ff), BF16),
            pltpu.VMEM((down_ring, local, depth, chunk), BF16),
            pltpu.VMEM((down_ring, count, chunk), F32),
            pltpu.VMEM((CHUNKS, n_e, group, chunk), BF16),
            pltpu.VMEM((CHUNKS, n_e - 1, group, chunk), BF16),
            pltpu.VMEM((n_dp, tok, span), F32),
            pltpu.VMEM((n_dp, tok, span), F32),
            sem((2, 4, max(sizes))), sem((2, 4, max(sizes))),
            sem((ring, 2)), sem((down_ring,)),
            sem((local, 2 * sizes[2])), sem((local, 2 * sizes[2])),
            sem((CHUNKS,)), sem((CHUNKS,)),
            sem((n_dp,)), sem((n_dp,)),
        ],
        compiler_params=pltpu.CompilerParams(
            collective_id=0, has_side_effects=True, vmem_limit_bytes=62 * 2**20
        ),
    )(tokens, routes, gate_scores, w_gate, w_up, w_down)


def solution(mesh):
    placed = (
        P(("dp", "expert"), None),
        P(("dp", "expert"), None),
        P(("dp", "expert"), None),
        P("expert", None, "dp"),
        P("expert", None, "dp"),
        P("expert", None, "dp"),
    )
    return jax.shard_map(
        body, mesh=mesh, in_specs=placed, out_specs=P(("dp", "expert"), None), check_vma=False
    )
```
